512 devices in a mesh: seq: 64 (over x, z), head: 8 (over y, core).
Axes of the slice: x: 4, y: 4, z: 16, core: 2. Of those that a mesh axis runs over, the one named last changes fastest.
Arguments:
- q_raw: bfloat16 [8192, 4096], P('seq', 'head'), may hold values from -6 to 6
- k_raw: bfloat16 [8192, 4096], P('seq', 'head'), may hold values from -6 to 6
- v_raw: bfloat16 [8192, 4096], P('seq', 'head'), may hold values from -7.5 to 7.5
- log_decay: bfloat16 [8192, 4096], P('seq', 'head'), may hold values from -0.7 to 0
- beta_logit: float32 [32, 8192], P('head', 'seq'), may hold values from -8 to 5
- conv_weight: float32 [3, 4, 4096], P(None, None, 'head'), may hold values from -3 to 3
- norm_gain: float32 [4096], P('head'), may hold values from 0.1 to 1.9
- out_weight: bfloat16 [4096, 2304], P('head'), may hold values from -0.09375 to 0.09375
Outputs:
- layer_out: bfloat16 [8192, 2304], P(('seq', 'head'))
The draws below stay inside these ranges and needn't reach their ends.
All inputs are finite; a program needn't handle non-finite values.
Results may differ from the reference program's by a relative error of at most 0.017.
Values may be sent and summed in bfloat16 or wider, within the bound.
A program may use at most 128 MiB of HBM per device.

```python
import jax
import jax.numpy as jnp
from jax import lax

D = 2304
HEAD_COUNT = 32
HEAD_WIDTH = 128
CONV = 4
BLOCK = 64
TOK_DEV = 128
TOKENS = 8192
N_HEAD = 8


def draw_log_decay(key, part):
    key = jax.random.fold_in(key, 11)
    key_sequence = jax.random.split(key, 7)
    columns = HEAD_COUNT * HEAD_WIDTH
    slow_count = 5
    slow_pick = jax.random.randint(key_sequence[0], (columns,), 0, 10) < slow_count
    fast_rate = jnp.exp(jax.random.uniform(key_sequence[1], (columns,), jnp.float32, jnp.log(1.0 / 50.0), jnp.log(1.0 / 30.0)))
    slow_rate = jnp.exp(jax.random.uniform(key_sequence[2], (columns,), jnp.float32, jnp.log(0.05), jnp.log(0.25))) / TOKENS
    base_rate = jnp.where(slow_pick, slow_rate, fast_rate)
    shard_count = TOKENS // TOK_DEV
    shard_factor = jnp.exp(jax.random.uniform(key_sequence[3], (shard_count, 1, columns), jnp.float32, jnp.log(0.5), jnp.log(2.0)))
    roughness = jnp.exp(jax.random.uniform(key_sequence[4], (shard_count, TOK_DEV, columns), jnp.float32, jnp.log(0.6), jnp.log(1.8)))
    steady_portion = -(base_rate * shard_factor * roughness).reshape(TOKENS, columns)
    third_term = TOKENS // 3
    spike_positions = jnp.arange(3, dtype=jnp.int32)[None, :] * third_term + jax.random.randint(key_sequence[5], (HEAD_COUNT, 3), 0, third_term)
    spike_decay_loss = jnp.log(1.0 - jax.random.uniform(key_sequence[6], (HEAD_COUNT, 3), jnp.float32, 0.2, 0.4))
    token_position = jnp.arange(TOKENS, dtype=jnp.int32)
    spike_lookup_table = (token_position[:, None, None] == spike_positions[None, :, :]).astype(jnp.float32)
    spike_portion = jnp.sum(spike_lookup_table * spike_decay_loss[None], axis=-1)
    spike_portion = jnp.repeat(spike_portion, HEAD_WIDTH, axis=1)
    return (steady_portion + spike_portion).astype(jnp.bfloat16)


def draw_v_raw(key, part):
    key = jax.random.fold_in(key, 23)
    key_sequence = jax.random.split(key, 2)
    columns = HEAD_COUNT * HEAD_WIDTH
    region_len = TOK_DEV // 2
    region_count = TOKENS // region_len
    base = jax.random.truncated_normal(key_sequence[0], -5.0, 5.0, (TOKENS, columns), jnp.float32)
    offset = 0.8 * jax.random.truncated_normal(key_sequence[1], -3.0, 3.0, (region_count, 1, columns), jnp.float32)
    shifted = base.reshape(region_count, region_len, columns) + offset
    return shifted.reshape(TOKENS, columns).astype(jnp.bfloat16)


def draw_beta_logit(key, part):
    key = jax.random.fold_in(key, 37)
    key_sequence = jax.random.split(key, 3)
    weak_count = 5
    weak_pick = jax.random.randint(key_sequence[0], (HEAD_COUNT, 1), 0, 10) < weak_count
    strong = 1.5 * jax.random.truncated_normal(key_sequence[1], -3.3, 3.3, (HEAD_COUNT, TOKENS), jnp.float32)
    weak = jax.random.uniform(key_sequence[2], (HEAD_COUNT, TOKENS), jnp.float32, -8.0, -6.5)
    return jnp.where(weak_pick, weak, strong)


def levels(stream_key, extent, shards, least, top_value):
    factor_of = 1.0
    for position, shards_of in shards:
        steps = jax.random.uniform(jax.random.fold_in(jax.random.fold_in(stream_key, 6), position), (shards_of,), jnp.float32, least / len(shards), top_value / len(shards))
        factor_of = factor_of * jnp.repeat(jnp.exp(steps), extent[position] // shards_of).reshape((-1,) + (1,) * (len(extent) - 1 - position))
    return factor_of


def bell_draw(stream_key, dims, width, limit, cuts=(), kind=jnp.bfloat16):
    result = jax.random.normal(stream_key, dims, jnp.float32) * width
    if len(cuts) > 0:
        result = levels(stream_key, dims, cuts, -0.22, 0.18) * result
    return jnp.clip(result, min=-limit, max=limit).astype(kind)


def setup_inputs(seed: int = 0) -> dict:
    key_of = jax.random.split(jax.random.key(seed), 9)
    return {
        "q_raw": bell_draw(key_of[0], (TOKENS, HEAD_COUNT * HEAD_WIDTH), 1.0, 6.0, ((0, 64), (1, 8))),
        "k_raw": bell_draw(key_of[1], (TOKENS, HEAD_COUNT * HEAD_WIDTH), 1.0, 6.0, ((0, 64), (1, 8))),
        "v_raw": draw_v_raw(jax.random.fold_in(key_of[8], 71), 0),
        "log_decay": draw_log_decay(jax.random.fold_in(key_of[8], 71), 0),
        "beta_logit": draw_beta_logit(jax.random.fold_in(key_of[8], 71), 0),
        "conv_weight": bell_draw(key_of[5], (3, CONV, HEAD_COUNT * HEAD_WIDTH), 0.5, 3.0, ((2, 8),), jnp.float32),
        "norm_gain": jnp.clip(1.0 + 0.18 * jax.random.normal(key_of[6], (HEAD_COUNT * HEAD_WIDTH,), jnp.float32), 0.1, 1.9),
        "out_weight": bell_draw(key_of[7], (HEAD_COUNT * HEAD_WIDTH, D), (HEAD_COUNT * HEAD_WIDTH) ** -0.5, 0.09375, ((0, 8),)),
    }


highest = lax.Precision.HIGHEST

def contract_product(pattern, left, right):
    return jnp.einsum(pattern, left, right, precision=highest)

def unit_rows(values_in):
    return values_in * lax.rsqrt(lax.optimization_barrier(jnp.sum(values_in * values_in, axis=-1, keepdims=True)) + 1e-06)

def conv_block(padded, conv_taps):
    out_len = padded.shape[0] - conv_taps.shape[0] + 1
    widened = padded.astype(jnp.float32)
    summed = jnp.zeros((out_len, widened.shape[1]), jnp.float32)
    for offset in range(conv_taps.shape[0]):
        summed = summed + widened[offset:offset + out_len] * conv_taps[offset]
    return jax.nn.silu(summed)

def block_terms(queries, keys_in, values_in, log_rate, strength):
    block_len = queries.shape[-2]
    filled = jnp.ones((block_len, block_len), jnp.float32)
    inclusive = jnp.tril(filled)
    strict = jnp.tril(filled, -1)
    cumulative = jnp.einsum('ts,...sk->...tk', inclusive, log_rate, precision=highest)
    last_row = cumulative[..., -1:, :]
    key_pos = keys_in * jnp.exp(cumulative)
    key_neg = keys_in * jnp.exp(-cumulative)
    query_position = queries * jnp.exp(cumulative)
    key_final_decay = keys_in * jnp.exp(last_row - cumulative)
    lower = contract_product('...tk,...sk->...ts', key_pos, key_neg) * strict
    attention_scores = contract_product('...tk,...sk->...ts', query_position, key_neg) * inclusive
    system = jnp.eye(block_len, dtype=jnp.float32) + strength[..., :, None] * lower
    right_side = strength[..., :, None] * jnp.concatenate([key_pos, values_in], axis=-1)
    solved = jax.scipy.linalg.solve_triangular(system, right_side, lower=True, unit_diagonal=True)
    key_width = keys_in.shape[-1]
    return (query_position, key_final_decay, jnp.exp(last_row), solved[..., :key_width], solved[..., key_width:], attention_scores)

def reference(q_raw, k_raw, v_raw, log_decay, beta_logit, conv_weight, norm_gain, out_weight):
    rim_len = CONV - 1
    feat_width = HEAD_COUNT * HEAD_WIDTH
    leading = jnp.zeros((rim_len, feat_width), jnp.bfloat16)
    padded_all = [jnp.concatenate([leading, source], axis=0) for source in (q_raw, k_raw, v_raw)]
    gain = norm_gain.reshape(HEAD_COUNT, 1, HEAD_WIDTH)

    def heads_first(matrix):
        return matrix.reshape(BLOCK, HEAD_COUNT, HEAD_WIDTH).transpose(1, 0, 2)

    def advance(memory_state, block_idx):
        first_row = block_idx * BLOCK
        convolved = [conv_block(lax.dynamic_slice_in_dim(padded_all[which], first_row, BLOCK + rim_len, 0), conv_weight[which]) for which in range(3)]
        queries = unit_rows(heads_first(convolved[0]))
        keys_in = unit_rows(heads_first(convolved[1]))
        values_in = heads_first(convolved[2])
        log_rate = heads_first(lax.dynamic_slice_in_dim(log_decay, first_row, BLOCK, 0).astype(jnp.float32))
        strength = jax.nn.sigmoid(lax.dynamic_slice_in_dim(beta_logit, first_row, BLOCK, 1))
        query_position, key_final_decay, final_decay, resolved_keys, resolved_values, attention_scores = block_terms(queries, keys_in, values_in, log_rate, strength)
        fresh_values = resolved_values - contract_product('xiy,xyp->xip', resolved_keys, memory_state)
        attention_output = contract_product('xiy,xyp->xip', query_position, memory_state) + contract_product('cpo,con->cpn', attention_scores, fresh_values)
        memory_state = jnp.swapaxes(final_decay, -1, -2) * memory_state + contract_product('rod,roq->rdq', key_final_decay, fresh_values)
        normed = attention_output * lax.rsqrt(lax.optimization_barrier(jnp.mean(attention_output * attention_output, axis=-1, keepdims=True)) + 1e-06) * gain
        return (memory_state, normed.transpose(1, 0, 2).reshape(BLOCK, feat_width).astype(jnp.bfloat16))
    start_memory = jnp.zeros((HEAD_COUNT, HEAD_WIDTH, HEAD_WIDTH), jnp.float32)
    _, blocks = lax.scan(advance, start_memory, jnp.arange(TOKENS // BLOCK, dtype=jnp.int32))
    normed_all = blocks.reshape(TOKENS, feat_width)
    group_width = feat_width // N_HEAD

    def add_group(index, summed):
        portion = lax.dynamic_slice_in_dim(normed_all, index * group_width, group_width, 1)
        weight_rows = lax.dynamic_slice_in_dim(out_weight, index * group_width, group_width, 0)
        partial_value = lax.optimization_barrier(jnp.dot(portion.astype(jnp.float32), weight_rows.astype(jnp.float32), preferred_element_type=jnp.float32).astype(jnp.bfloat16))
        return summed + partial_value.astype(jnp.float32)
    summed = lax.fori_loop(0, N_HEAD, add_group, jnp.zeros((TOKENS, D), jnp.float32))
    return summed.astype(jnp.bfloat16)
```

```python
import functools

import jax
import jax.numpy as jnp
from jax import lax
from jax.experimental import pallas as pl
from jax.experimental.pallas import tpu as pltpu
from jax.sharding import PartitionSpec as P

MESH = pl.DeviceIdType.MESH
F32 = jnp.float32
BF16 = jnp.bfloat16
HW = 128
CONV = 4
RIM = 16
CHUNKS = 3


def halves(value):
    high = value.astype(BF16)
    return high, (value - high.astype(F32)).astype(BF16)


def mm(a, b):
    return jnp.dot(a, b, preferred_element_type=F32)


def mm_full(a, b):
    a_hi, a_lo = halves(a)
    b_hi, b_lo = halves(b)
    wide = mm(jnp.concatenate([a_hi, a_lo], axis=1), jnp.concatenate([b_hi, b_hi], axis=0))
    return wide + mm(a_hi, b_lo)


def mm_exact_left(a_bf, b):
    b_hi, b_lo = halves(b)
    return mm(jnp.concatenate([a_bf, a_bf], axis=1), jnp.concatenate([b_hi, b_lo], axis=0))


def iotas(n):
    return lax.broadcasted_iota(jnp.int32, (n, n), 0), lax.broadcasted_iota(jnp.int32, (n, n), 1)


def unit_lower_inverses(lowers, row, col):
    differ = jnp.bitwise_xor(row, col)
    eye = (row == col).astype(F32)
    invs = [eye - jnp.where(differ == 1, low, 0.0) for low in lowers]
    level = 1
    while (2 << level) <= lowers[0].shape[0]:
        pick = lax.shift_right_logical(differ, level) == 1
        mids = [mm_full(jnp.where(pick, low, 0.0), inv) for low, inv in zip(lowers, invs)]
        invs = [inv - mm_full(inv, mid) for inv, mid in zip(invs, mids)]
        level += 1
    return invs


def compose(later_bf, earlier):
    width = earlier.shape[0]
    return earlier + mm_exact_left(later_bf[:, :width], earlier) + later_bf.astype(F32)


def kernel(
    q_hbm, k_hbm, v_hbm, ld_hbm, beta_hbm, taps_hbm, gain_hbm, w_hbm,
    o_ref,
    q_in, k_in, v_in, ld_in, beta_in, taps_in, gain_in, w_in,
    rims, ext, qeff, intra,
    e1_send, e1_recv, e2_send, e2_recv, e3_send, e3_recv, s4_send, s4_recv,
    parts, landed,
    local_sem, rim_send, rim_recv,
    l1s, l1r, l2s, l2r, l3s, l3r, l4s, l4r, rss, rsr,
):
    seq, head = lax.axis_index("seq"), lax.axis_index("head")
    seqs, heads = 64, 8
    x, a, b = seq // 16, (seq // 4) % 4, seq % 4
    toks, feat = q_in.shape
    local_heads = feat // HW

    sources = (q_hbm, k_hbm, v_hbm, ld_hbm, beta_hbm, taps_hbm, gain_hbm, w_hbm)
    inside = (q_in, k_in, v_in, ld_in, beta_in, taps_in, gain_in, w_in)
    loads = [
        pltpu.make_async_copy(src, dst, local_sem.at[i])
        for i, (src, dst) in enumerate(zip(sources, inside))
    ]
    for load in loads:
        load.start()

    def at1(d):
        return seq - b + (b + d) % 4

    def at2(d):
        return seq - 4 * a + 4 * ((a + d) % 4)

    def at3(d):
        return seq - 16 * x + 16 * ((x + d) % 4)

    after, before = (seq + 1) % seqs, (seq + seqs - 1) % seqs
    barrier = pltpu.get_barrier_semaphore()
    greet = [(after, head), (before, head)]
    greet += [(at(d), head) for at in (at1, at2, at3) for d in (1, 2, 3)]
    greet += [(seq, (head + d) % heads) for d in range(1, heads)]
    for device in greet:
        pl.semaphore_signal(barrier, inc=1, device_id=device, device_id_type=MESH)
    pl.semaphore_wait(barrier, len(greet))

    def remote(src, dst, send, recv, device):
        return pltpu.make_async_remote_copy(
            src_ref=src, dst_ref=dst, send_sem=send, recv_sem=recv, device_id=device, device_id_type=MESH
        )

    rim_copies = [
        remote(src.at[pl.ds(toks - RIM, RIM), :], rims.at[i], rim_send.at[i], rim_recv.at[i], (after, head))
        for i, src in enumerate((q_hbm, k_hbm, v_hbm))
    ]
    for copy in rim_copies:
        copy.start()

    row, col = iotas(toks)
    inclusive = row >= col
    strict = row > col
    eye = (row == col).astype(F32)
    for load in loads[3:7]:
        load.wait()
    cum = mm(inclusive.astype(BF16), ld_in[...])
    middle = cum[toks // 2 - 1 : toks // 2, :]
    last = cum[toks - 1 : toks, :]
    grow = jnp.exp(cum - middle)
    shrink = jnp.exp(middle - cum)
    from_start = jnp.exp(middle)
    to_end = jnp.exp(last - middle)
    loss = jnp.exp(last) - 1.0
    strength = 1.0 / (1.0 + jnp.exp(-beta_in[...]))

    conved = []
    for load in loads[:3]:
        load.wait()
    for copy in rim_copies:
        copy.wait_recv()
    for i, inp in enumerate((q_in, k_in, v_in)):
        ext[i, 0:RIM, :] = jnp.where(seq > 0, rims[i].astype(F32), 0.0)
        ext[i, RIM : RIM + toks, :] = inp[...].astype(F32)
        total = jnp.zeros((toks, feat), F32)
        for j in range(CONV):
            first = RIM - (CONV - 1) + j
            total = total + ext[i, first : first + toks, :] * taps_in[i, j : j + 1, :]
        conved.append(total / (1.0 + jnp.exp(-total)))

    queries, keys, values, lowers, scores, betas = [], [], [], [], [], []
    for h in range(local_heads):
        cols = slice(h * HW, (h + 1) * HW)
        q_h, k_h, v_h = (part[:, cols] for part in conved)
        q_h = q_h * lax.rsqrt(jnp.sum(q_h * q_h, axis=-1, keepdims=True) + 1e-06)
        k_h = k_h * lax.rsqrt(jnp.sum(k_h * k_h, axis=-1, keepdims=True) + 1e-06)
        beta = jnp.transpose(jnp.broadcast_to(strength[h : h + 1, :], (HW, toks)))
        key_pos, key_neg, query_pos = k_h * grow[:, cols], k_h * shrink[:, cols], q_h * grow[:, cols]
        both = mm_full(jnp.concatenate([key_pos, query_pos], axis=0), jnp.transpose(key_neg))
        lowers.append(jnp.where(strict, both[:toks] * beta, 0.0))
        scores.append(jnp.where(inclusive, both[toks:], 0.0))
        queries.append(query_pos * from_start[:, cols])
        keys.append(jnp.transpose(key_neg * to_end[:, cols]))
        values.append(jnp.concatenate([key_pos * from_start[:, cols] * beta, v_h * beta], axis=1))
    inverses = unit_lower_inverses(lowers, row, col)
    solved = [mm_full(inv, rhs) for inv, rhs in zip(inverses, values)]
    for h in range(local_heads):
        cols = slice(h * HW, (h + 1) * HW)
        outs = mm_full(jnp.concatenate([scores[h], keys[h]], axis=0), solved[h])
        qeff[h] = queries[h] - outs[:toks, :HW]
        intra[h] = outs[:toks, HW:]
        e1_send[h, :, :HW] = (eye * loss[:, cols] - outs[toks:, :HW]).astype(BF16)
        e1_send[h, :, HW:] = outs[toks:, HW:].astype(BF16)

    def exchange(send_of, recv, mine, at, sends, recvs):
        out, arrive = [], []
        for d in (1, 2, 3):
            copy = remote(send_of((mine + d) % 4), recv.at[mine], sends.at[d - 1], recvs.at[d - 1], (at(d), head))
            copy.start()
            out.append(copy)
            slot = (mine + 4 - d) % 4
            arrive.append(remote(send_of(slot), recv.at[slot], sends.at[d - 1], recvs.at[d - 1], (at(d), head)))
        return out, arrive

    out1, arrive1 = exchange(lambda h: e1_send.at[h], e1_recv, b, at1, l1s, l1r)
    e1_recv[b] = e1_send[b]
    for copy in arrive1:
        copy.wait_recv()
    maps1 = [e1_recv[0].astype(F32)]
    for n in (1, 2, 3):
        maps1.append(compose(e1_recv[n], maps1[-1]))

    e2_send[...] = maps1[3].astype(BF16)
    out2, arrive2 = exchange(lambda h: e2_send, e2_recv, a, at2, l2s, l2r)
    e2_recv[a] = e2_send[...]
    for copy in arrive2:
        copy.wait_recv()
    run = e2_recv[0].astype(F32)
    before2 = jnp.zeros_like(run)
    for n in (1, 2, 3):
        before2 = jnp.where(a == n, run, before2)
        run = compose(e2_recv[n], run)

    e3_send[...] = run.astype(BF16)
    out3, arrive3 = exchange(lambda h: e3_send, e3_recv, x, at3, l3s, l3r)
    for copy in arrive3:
        copy.wait_recv()
    state = e3_recv[0, :, HW:].astype(F32)
    entering = jnp.zeros_like(state)
    entering = jnp.where(x == 1, state, entering)
    for n in (1, 2):
        state = state + mm_exact_left(e3_recv[n, :, :HW], state) + e3_recv[n, :, HW:].astype(F32)
        entering = jnp.where(x == n + 1, state, entering)
    entering = entering + mm_full(before2[:, :HW], entering) + before2[:, HW:]
    s4_send[0] = entering.astype(BF16)
    for n in (1, 2, 3):
        s4_send[n] = (entering + mm_full(maps1[n - 1][:, :HW], entering) + maps1[n - 1][:, HW:]).astype(BF16)

    out4, arrive4 = exchange(lambda h: s4_send.at[h], s4_recv, b, at1, l4s, l4r)
    s4_recv[b] = s4_send[b]
    for copy in arrive4:
        copy.wait_recv()
    normed = []
    for h in range(local_heads):
        q_hi, q_lo = halves(qeff[h])
        state_h = s4_recv[h]
        attended = intra[h] + mm(
            jnp.concatenate([q_hi, q_lo], axis=1), jnp.concatenate([state_h, state_h], axis=0)
        )
        scale = lax.rsqrt(jnp.mean(attended * attended, axis=-1, keepdims=True) + 1e-06)
        normed.append((attended * scale * gain_in[:, h * HW : (h + 1) * HW]).astype(BF16))
    normed = jnp.concatenate(normed, axis=1)

    loads[7].wait()
    width = w_in.shape[1] // CHUNKS
    rows = toks // heads
    sent, coming = [], []
    for c in range(CHUNKS):
        cols = slice(c * width, (c + 1) * width)
        partial = mm(normed, w_in[:, cols]).astype(BF16)
        for t in range(heads):
            parts[t, :, cols] = partial[t * rows : (t + 1) * rows]
        for d in range(1, heads):
            to, source = (head + d) % heads, (head + heads - d) % heads
            at = pl.ds(c * width, width)
            copy = remote(
                parts.at[to, :, at], landed.at[head, :, at], rss.at[c, d - 1], rsr.at[c, d - 1], (seq, to)
            )
            copy.start()
            sent.append(copy)
            coming.append(
                remote(
                    parts.at[to, :, at], landed.at[source, :, at], rss.at[c, d - 1], rsr.at[c, d - 1], (seq, to)
                )
            )
    for c in range(CHUNKS):
        cols = slice(c * width, (c + 1) * width)
        summed = parts[head, :, cols].astype(F32)
        for d in range(1, heads):
            coming[c * (heads - 1) + d - 1].wait_recv()
            summed = summed + landed[(head + heads - d) % heads, :, cols].astype(F32)
        o_ref[:, cols] = summed.astype(BF16)
    for copy in rim_copies + out1 + out2 + out3 + out4 + sent:
        copy.wait_send()


def body(q_raw, k_raw, v_raw, log_decay, beta_logit, conv_weight, norm_gain, out_weight):
    toks, feat = q_raw.shape
    local_heads = feat // HW
    heads = lax.axis_size("head")
    width = out_weight.shape[1]
    dma = pltpu.SemaphoreType.DMA
    gain = norm_gain.reshape(1, feat)
    operands = (q_raw, k_raw, v_raw, log_decay, beta_logit, conv_weight, gain, out_weight)
    scratch = [pltpu.VMEM(op.shape, op.dtype) for op in operands]
    scratch += [
        pltpu.VMEM((3, RIM, feat), BF16),
        pltpu.VMEM((3, RIM + toks, feat), F32),
        pltpu.VMEM((local_heads, toks, HW), F32),
        pltpu.VMEM((local_heads, toks, HW), F32),
        pltpu.VMEM((4, HW, 2 * HW), BF16),
        pltpu.VMEM((4, HW, 2 * HW), BF16),
        pltpu.VMEM((HW, 2 * HW), BF16),
        pltpu.VMEM((4, HW, 2 * HW), BF16),
        pltpu.VMEM((HW, 2 * HW), BF16),
        pltpu.VMEM((4, HW, 2 * HW), BF16),
        pltpu.VMEM((4, HW, HW), BF16),
        pltpu.VMEM((4, HW, HW), BF16),
        pltpu.VMEM((heads, toks // heads, width), BF16),
        pltpu.VMEM((heads, toks // heads, width), BF16),
        dma((len(operands),)), dma((3,)), dma((3,)),
        dma((3,)), dma((3,)), dma((3,)), dma((3,)), dma((3,)), dma((3,)), dma((3,)), dma((3,)),
        dma((CHUNKS, heads - 1)), dma((CHUNKS, heads - 1)),
    ]
    return pl.pallas_call(
        kernel,
        out_shape=jax.ShapeDtypeStruct((toks // heads, width), BF16),
        in_specs=[pl.BlockSpec(memory_space=pl.ANY)] * len(operands),
        out_specs=pl.BlockSpec(memory_space=pltpu.VMEM),
        scratch_shapes=scratch,
        compiler_params=pltpu.CompilerParams(
            collective_id=0, has_side_effects=True, vmem_limit_bytes=48 * 2**20
        ),
        cost_estimate=pl.CostEstimate(flops=2 * 10**9, bytes_accessed=3 * 10**6, transcendentals=10**6),
    )(*operands)


def solution(mesh):
    in_specs = (
        P("seq", "head"),
        P("seq", "head"),
        P("seq", "head"),
        P("seq", "head"),
        P("head", "seq"),
        P(None, None, "head"),
        P("head"),
        P("head", None),
    )
    out_specs = P(("seq", "head"), None)
    return jax.shard_map(body, mesh=mesh, in_specs=in_specs, out_specs=out_specs, check_vma=False)
```

```python
import functools

import jax
import jax.numpy as jnp
from jax import lax
from jax.experimental import pallas as pl
from jax.experimental.pallas import tpu as pltpu
from jax.sharding import PartitionSpec as P

MESH = pl.DeviceIdType.MESH
F32 = jnp.float32
BF16 = jnp.bfloat16
HW = 128
CONV = 4
RIM = 16
EDGE = 8
CHUNKS = 3


def halves(value):
    high = value.astype(BF16)
    return high, (value - high.astype(F32)).astype(BF16)


def mm(a, b):
    return jnp.dot(a, b, preferred_element_type=F32)


def mm_full(a, b):
    a_hi, a_lo = halves(a)
    b_hi, b_lo = halves(b)
    wide = mm(jnp.concatenate([a_hi, a_lo], axis=1), jnp.concatenate([b_hi, b_hi], axis=0))
    return wide + mm(a_hi, b_lo)


def mm_exact_left(a_bf, b):
    b_hi, b_lo = halves(b)
    return mm(jnp.concatenate([a_bf, a_bf], axis=1), jnp.concatenate([b_hi, b_lo], axis=0))


def iotas(n):
    return lax.broadcasted_iota(jnp.int32, (n, n), 0), lax.broadcasted_iota(jnp.int32, (n, n), 1)


def unit_lower_inverses(lowers, row, col):
    differ = jnp.bitwise_xor(row, col)
    eye = (row == col).astype(F32)
    invs = [eye - jnp.where(differ == 1, low, 0.0) for low in lowers]
    level = 1
    while (2 << level) <= lowers[0].shape[0]:
        pick = lax.shift_right_logical(differ, level) == 1
        mids = [mm_full(jnp.where(pick, low, 0.0), inv) for low, inv in zip(lowers, invs)]
        invs = [inv - mm_full(inv, mid) for inv, mid in zip(invs, mids)]
        level += 1
    return invs


def conv_silu(ext, taps, i, rows):
    total = jnp.zeros((rows, ext.shape[2]), F32)
    for j in range(CONV):
        first = RIM - (CONV - 1) + j
        total = total + ext[i, first : first + rows, :] * taps[i, j : j + 1, :]
    return total / (1.0 + jnp.exp(-total))


def compose(later_bf, earlier):
    width = earlier.shape[0]
    return earlier + mm_exact_left(later_bf[:, :width], earlier) + later_bf.astype(F32)


def kernel(
    q_hbm, k_hbm, v_hbm, ld_hbm, beta_hbm, taps_hbm, gain_hbm, w_hbm,
    o_ref,
    q_in, k_in, v_in, ld_in, beta_in, taps_in, gain_in, w_in,
    rims, ext, qeff, intra,
    e1_send, e1_recv, e2_send, e2_recv, n3_send, n3_recv, e3_send, e3_recv, s4_send, s4_recv,
    parts, paired, summed, landed,
    local_sem, rim_send, rim_recv,
    l1s, l1r, l2s, l2r, l3s, l3r, l4s, l4r, prs, prr, rss, rsr,
):
    seq, head = lax.axis_index("seq"), lax.axis_index("head")
    seqs, heads = 64, 8
    x, a, b = seq // 16, (seq // 4) % 4, seq % 4
    toks, feat = q_in.shape
    local_heads = feat // HW

    sources = (q_hbm, k_hbm, v_hbm, ld_hbm, beta_hbm, taps_hbm, gain_hbm, w_hbm)
    inside = (q_in, k_in, v_in, ld_in, beta_in, taps_in, gain_in, w_in)
    loads = [
        pltpu.make_async_copy(src, dst, local_sem.at[i])
        for i, (src, dst) in enumerate(zip(sources, inside))
    ]
    for load in loads:
        load.start()

    other = head + 1 - 2 * (head % 2)

    def across(d):
        return (head + 2 * d) % heads

    def at1(d):
        return seq - b + (b + d) % 4

    def at2(d):
        return seq - 4 * a + 4 * ((a + d) % 4)

    def at3(d):
        return seq - 16 * x + 16 * ((x + d) % 4)

    after, before = (seq + 1) % seqs, (seq + seqs - 1) % seqs
    barrier = pltpu.get_barrier_semaphore()
    greet = [(after, head), (before, head)]
    greet += [(at(d), head) for at in (at1, at2, at3) for d in (1, 2, 3)]
    greet += [(seq, other)] + [(seq, across(d)) for d in (1, 2, 3)]
    for device in greet:
        pl.semaphore_signal(barrier, inc=1, device_id=device, device_id_type=MESH)

    def remote(src, dst, send, recv, device):
        return pltpu.make_async_remote_copy(
            src_ref=src, dst_ref=dst, send_sem=send, recv_sem=recv, device_id=device, device_id_type=MESH
        )

    row, col = iotas(toks)
    inclusive = row >= col
    strict = row > col
    eye = (row == col).astype(F32)
    for load in loads[3:7]:
        load.wait()
    cum = mm(inclusive.astype(BF16), ld_in[...])
    middle = cum[toks // 2 - 1 : toks // 2, :]
    last = cum[toks - 1 : toks, :]
    grow = jnp.exp(cum - middle)
    shrink = jnp.exp(middle - cum)
    from_start = jnp.exp(middle)
    to_end = jnp.exp(last - middle)
    loss = jnp.exp(last) - 1.0
    strength = 1.0 / (1.0 + jnp.exp(-beta_in[...]))

    for load in loads[:3]:
        load.wait()
    raws = (q_in, k_in, v_in)
    for i in range(3):
        ext[i, 0:RIM, :] = jnp.zeros((RIM, feat), F32)
        ext[i, RIM : RIM + toks, :] = raws[i][...].astype(F32)
    conved = [conv_silu(ext, taps_in, i, toks) for i in range(3)]

    pl.semaphore_wait(barrier, len(greet))
    rim_copies = [
        remote(src.at[pl.ds(toks - RIM, RIM), :], rims.at[i], rim_send.at[i], rim_recv.at[i], (after, head))
        for i, src in enumerate((q_hbm, k_hbm, v_hbm))
    ]
    for copy in rim_copies:
        copy.start()

    def head_parts(parts_of, h, rows):
        cols = slice(h * HW, (h + 1) * HW)
        q_h, k_h, v_h = (part[:, cols] for part in parts_of)
        q_h = q_h * lax.rsqrt(jnp.sum(q_h * q_h, axis=-1, keepdims=True) + 1e-06)
        k_h = k_h * lax.rsqrt(jnp.sum(k_h * k_h, axis=-1, keepdims=True) + 1e-06)
        return k_h * grow[:rows, cols], k_h * shrink[:rows, cols], q_h * grow[:rows, cols], v_h

    betas, firsts, lowers = [], [], []
    for h in range(local_heads):
        betas.append(jnp.transpose(jnp.broadcast_to(strength[h : h + 1, :], (HW, toks))))
        firsts.append(head_parts(conved, h, toks))
        lower = mm_full(firsts[h][0], jnp.transpose(firsts[h][1])) * betas[h]
        lowers.append(jnp.where(strict & (col >= EDGE), lower, 0.0))
    inverses = unit_lower_inverses(lowers, row, col)

    for copy in rim_copies:
        copy.wait_recv()
    for i in range(3):
        ext[i, 0:RIM, :] = jnp.where(seq > 0, rims[i].astype(F32), 0.0)
    edges = [conv_silu(ext, taps_in, i, EDGE) for i in range(3)]
    queries, keys, scores, sides, corners = [], [], [], [], []
    for h in range(local_heads):
        cols = slice(h * HW, (h + 1) * HW)
        key_pos, key_neg, query_pos, v_h = (
            jnp.concatenate([edge, part[EDGE:]], axis=0)
            for edge, part in zip(head_parts(edges, h, EDGE), firsts[h])
        )
        both = mm_full(jnp.concatenate([key_pos, query_pos], axis=0), jnp.transpose(key_neg))
        corners.append(jnp.where(strict & (col < EDGE), both[:toks] * betas[h], 0.0))
        scores.append(jnp.where(inclusive, both[toks:], 0.0))
        queries.append(query_pos * from_start[:, cols])
        keys.append(jnp.transpose(key_neg * to_end[:, cols]))
        sides.append(jnp.concatenate([key_pos * from_start[:, cols] * betas[h], v_h * betas[h]], axis=1))
    edge_sols = [side[:EDGE] for side in sides]
    for j in range(EDGE - 1):
        edge_sols = [
            sol - corner[:EDGE, j : j + 1] * sol[j : j + 1, :] for sol, corner in zip(edge_sols, corners)
        ]
    below = [
        mm_full(corner, jnp.concatenate([sol, jnp.zeros((toks - EDGE, 2 * HW), F32)], axis=0))
        for corner, sol in zip(corners, edge_sols)
    ]
    solved = [
        mm_full(inv, jnp.concatenate([sol, side[EDGE:] - low[EDGE:]], axis=0))
        for inv, sol, side, low in zip(inverses, edge_sols, sides, below)
    ]
    for h in range(local_heads):
        cols = slice(h * HW, (h + 1) * HW)
        outs = mm_full(jnp.concatenate([scores[h], keys[h]], axis=0), solved[h])
        qeff[h] = queries[h] - outs[:toks, :HW]
        intra[h] = outs[:toks, HW:]
        e1_send[h, :, :HW] = (eye * loss[:, cols] - outs[toks:, :HW]).astype(BF16)
        e1_send[h, :, HW:] = outs[toks:, HW:].astype(BF16)

    def exchange(send_of, recv, mine, at, sends, recvs):
        out, arrive = [], []
        for d in (2, 1, 3):
            copy = remote(send_of((mine + d) % 4), recv.at[mine], sends.at[d - 1], recvs.at[d - 1], (at(d), head))
            copy.start()
            out.append(copy)
            slot = (mine + 4 - d) % 4
            arrive.append(remote(send_of(slot), recv.at[slot], sends.at[d - 1], recvs.at[d - 1], (at(d), head)))
        return out, arrive

    out1, arrive1 = exchange(lambda h: e1_send.at[h], e1_recv, b, at1, l1s, l1r)
    e1_recv[b] = e1_send[b]
    for copy in arrive1:
        copy.wait_recv()
    maps1 = [e1_recv[0].astype(F32)]
    for n in (1, 2, 3):
        maps1.append(compose(e1_recv[n], maps1[-1]))

    e2_send[...] = maps1[3].astype(BF16)
    out2, arrive2 = exchange(lambda h: e2_send, e2_recv, a, at2, l2s, l2r)
    e2_recv[a] = e2_send[...]
    for copy in arrive2:
        copy.wait_recv()
    run = e2_recv[0].astype(F32)
    before2 = jnp.zeros_like(run)
    for n in (1, 2, 3):
        before2 = jnp.where(a == n, run, before2)
        run = compose(e2_recv[n], run)

    n3_send[...] = run[:, HW:].astype(BF16)
    e3_send[...] = run[:, :HW].astype(BF16)
    out3n = [remote(n3_send, n3_recv.at[x], l3s.at[d - 1], l3r.at[d - 1], (at3(d), head)) for d in (1, 2, 3)]
    out3e = [remote(e3_send, e3_recv.at[x], l3s.at[d + 2], l3r.at[d + 2], (at3(d), head)) for d in (1, 2)]
    came3n = [
        remote(n3_send, n3_recv.at[(x + 4 - d) % 4], l3s.at[d - 1], l3r.at[d - 1], (at3(d), head)) for d in (1, 2, 3)
    ]
    came3e = [
        remote(e3_send, e3_recv.at[(x + 4 - d) % 4], l3s.at[d + 2], l3r.at[d + 2], (at3(d), head)) for d in (1, 2)
    ]
    for d in (2, 1, 3):
        pl.when(x + d < 4)(out3n[d - 1].start)
    for d in (2, 1):
        pl.when((x >= 1) & (x + d < 4))(out3e[d - 1].start)
    for d in (1, 2, 3):
        pl.when(x >= d)(came3n[d - 1].wait_recv)
    for d in (1, 2):
        pl.when(x >= d + 1)(came3e[d - 1].wait_recv)
    state = n3_recv[0].astype(F32)
    entering = jnp.zeros_like(state)
    entering = jnp.where(x == 1, state, entering)
    for n in (1, 2):
        state = state + mm_exact_left(e3_recv[n], state) + n3_recv[n].astype(F32)
        entering = jnp.where(x == n + 1, state, entering)
    entering = entering + mm_full(before2[:, :HW], entering) + before2[:, HW:]
    s4_send[0] = entering.astype(BF16)
    for n in (1, 2, 3):
        s4_send[n] = (entering + mm_full(maps1[n - 1][:, :HW], entering) + maps1[n - 1][:, HW:]).astype(BF16)

    out4, arrive4 = exchange(lambda h: s4_send.at[h], s4_recv, b, at1, l4s, l4r)
    s4_recv[b] = s4_send[b]
    for copy in arrive4:
        copy.wait_recv()
    normed = []
    for h in range(local_heads):
        q_hi, q_lo = halves(qeff[h])
        state_h = s4_recv[h]
        attended = intra[h] + mm(
            jnp.concatenate([q_hi, q_lo], axis=1), jnp.concatenate([state_h, state_h], axis=0)
        )
        scale = lax.rsqrt(jnp.mean(attended * attended, axis=-1, keepdims=True) + 1e-06)
        normed.append((attended * scale * gain_in[:, h * HW : (h + 1) * HW]).astype(BF16))
    normed = jnp.concatenate(normed, axis=1)

    loads[7].wait()
    width = w_in.shape[1] // CHUNKS
    rows = toks // heads
    core, place = head % 2, head // 2
    pairs, spread, coming = [], [], []
    for c in range(CHUNKS):
        cols = slice(c * width, (c + 1) * width)
        partial = mm(normed, w_in[:, cols]).astype(BF16)
        for t in range(heads):
            parts[t % 2, (t // 2) * rows : (t // 2 + 1) * rows, cols] = partial[t * rows : (t + 1) * rows]
        copy = remote(parts.at[1 - core, :, cols], paired.at[:, cols], prs.at[c], prr.at[c], (seq, other))
        copy.start()
        pairs.append(copy)
    for c in range(CHUNKS):
        cols = slice(c * width, (c + 1) * width)
        pairs[c].wait_recv()
        both = parts[core, :, cols].astype(F32) + paired[:, cols].astype(F32)
        for t in range(4):
            summed[t, :, cols] = both[t * rows : (t + 1) * rows].astype(BF16)
        for d in (2, 1, 3):
            to, source = (place + d) % 4, (place + 4 - d) % 4
            ends = (rss.at[c, d - 1], rsr.at[c, d - 1], (seq, across(d)))
            copy = remote(summed.at[to, :, cols], landed.at[place, :, cols], *ends)
            copy.start()
            spread.append(copy)
            coming.append(remote(summed.at[to, :, cols], landed.at[source, :, cols], *ends))
    for c in range(CHUNKS):
        cols = slice(c * width, (c + 1) * width)
        total = summed[place, :, cols].astype(F32)
        for copy in coming[3 * c : 3 * c + 3]:
            copy.wait_recv()
        for d in (1, 2, 3):
            total = total + landed[(place + d) % 4, :, cols].astype(F32)
        o_ref[:, cols] = total.astype(BF16)
    for copy in rim_copies + out1 + out2 + out4 + pairs + spread:
        copy.wait_send()
    for d in (1, 2, 3):
        pl.when(x + d < 4)(out3n[d - 1].wait_send)
    for d in (1, 2):
        pl.when((x >= 1) & (x + d < 4))(out3e[d - 1].wait_send)


def body(q_raw, k_raw, v_raw, log_decay, beta_logit, conv_weight, norm_gain, out_weight):
    toks, feat = q_raw.shape
    local_heads = feat // HW
    heads = lax.axis_size("head")
    width = out_weight.shape[1]
    dma = pltpu.SemaphoreType.DMA
    gain = norm_gain.reshape(1, feat)
    operands = (q_raw, k_raw, v_raw, log_decay, beta_logit, conv_weight, gain, out_weight)
    scratch = [pltpu.VMEM(op.shape, op.dtype) for op in operands]
    scratch += [
        pltpu.VMEM((3, RIM, feat), BF16),
        pltpu.VMEM((3, RIM + toks, feat), F32),
        pltpu.VMEM((local_heads, toks, HW), F32),
        pltpu.VMEM((local_heads, toks, HW), F32),
        pltpu.VMEM((4, HW, 2 * HW), BF16),
        pltpu.VMEM((4, HW, 2 * HW), BF16),
        pltpu.VMEM((HW, 2 * HW), BF16),
        pltpu.VMEM((4, HW, 2 * HW), BF16),
        pltpu.VMEM((HW, HW), BF16),
        pltpu.VMEM((4, HW, HW), BF16),
        pltpu.VMEM((HW, HW), BF16),
        pltpu.VMEM((4, HW, HW), BF16),
        pltpu.VMEM((4, HW, HW), BF16),
        pltpu.VMEM((4, HW, HW), BF16),
        pltpu.VMEM((2, toks // 2, width), BF16),
        pltpu.VMEM((toks // 2, width), BF16),
        pltpu.VMEM((4, toks // heads, width), BF16),
        pltpu.VMEM((4, toks // heads, width), BF16),
        dma((len(operands),)), dma((3,)), dma((3,)),
        dma((3,)), dma((3,)), dma((3,)), dma((3,)), dma((5,)), dma((5,)), dma((3,)), dma((3,)),
        dma((CHUNKS,)), dma((CHUNKS,)), dma((CHUNKS, 3)), dma((CHUNKS, 3)),
    ]
    return pl.pallas_call(
        kernel,
        out_shape=jax.ShapeDtypeStruct((toks // heads, width), BF16),
        in_specs=[pl.BlockSpec(memory_space=pltpu.HBM)] * len(operands),
        out_specs=pl.BlockSpec(memory_space=pltpu.VMEM),
        scratch_shapes=scratch,
        compiler_params=pltpu.CompilerParams(
            collective_id=0, has_side_effects=True, vmem_limit_bytes=48 * 2**20
        ),
        cost_estimate=pl.CostEstimate(flops=2 * 10**9, bytes_accessed=3 * 10**6, transcendentals=10**6),
    )(*[pltpu.with_memory_space_constraint(op, pltpu.HBM) for op in operands])


def solution(mesh):
    in_specs = (
        P("seq", "head"),
        P("seq", "head"),
        P("seq", "head"),
        P("seq", "head"),
        P("head", "seq"),
        P(None, None, "head"),
        P("head"),
        P("head", None),
    )
    out_specs = P(("seq", "head"), None)
    return jax.shard_map(body, mesh=mesh, in_specs=in_specs, out_specs=out_specs, check_vma=False)
```

```python
import functools

import jax
import jax.numpy as jnp
from jax import lax
from jax.experimental import pallas as pl
from jax.experimental.pallas import tpu as pltpu
from jax.sharding import PartitionSpec as P

MESH = pl.DeviceIdType.MESH
F32 = jnp.float32
BF16 = jnp.bfloat16
HW = 128
CONV = 4
RIM = 16
EDGE = 8
CHUNKS = 1


def halves(value):
    high = value.astype(BF16)
    return high, (value - high.astype(F32)).astype(BF16)


def mm(a, b):
    return jnp.dot(a, b, preferred_element_type=F32)


def mm_full(a, b):
    a_hi, a_lo = halves(a)
    b_hi, b_lo = halves(b)
    wide = mm(jnp.concatenate([a_hi, a_lo], axis=1), jnp.concatenate([b_hi, b_hi], axis=0))
    return wide + mm(a_hi, b_lo)


def mm_exact_left(a_bf, b):
    b_hi, b_lo = halves(b)
    return mm(jnp.concatenate([a_bf, a_bf], axis=1), jnp.concatenate([b_hi, b_lo], axis=0))


def iotas(n):
    return lax.broadcasted_iota(jnp.int32, (n, n), 0), lax.broadcasted_iota(jnp.int32, (n, n), 1)


def unit_lower_inverses(lowers, row, col):
    differ = jnp.bitwise_xor(row, col)
    eye = (row == col).astype(F32)
    invs = [eye - jnp.where(differ == 1, low, 0.0) for low in lowers]
    level = 1
    while (2 << level) <= lowers[0].shape[0]:
        pick = lax.shift_right_logical(differ, level) == 1
        mids = [mm_full(jnp.where(pick, low, 0.0), inv) for low, inv in zip(lowers, invs)]
        invs = [inv - mm_full(inv, mid) for inv, mid in zip(invs, mids)]
        level += 1
    return invs


def conv_silu(ext, taps, i, rows):
    total = jnp.zeros((rows, ext.shape[2]), F32)
    for j in range(CONV):
        first = RIM - (CONV - 1) + j
        total = total + ext[i, first : first + rows, :] * taps[i, j : j + 1, :]
    return total / (1.0 + jnp.exp(-total))


def compose(later_bf, earlier):
    width = earlier.shape[0]
    return earlier + mm_exact_left(later_bf[:, :width], earlier) + later_bf.astype(F32)


def kernel(
    q_hbm, k_hbm, v_hbm, ld_hbm, beta_hbm, taps_hbm, gain_hbm, w_hbm,
    o_ref,
    q_in, k_in, v_in, ld_in, beta_in, taps_in, gain_in, w_in,
    rims, ext, qeff, intra,
    e1_send, e1_recv, e2_send, e2_recv, n3_send, n3_recv, e3_send, e3_recv, s4_send, s4_recv,
    parts, paired, summed, landed,
    local_sem, rim_send, rim_recv,
    l1s, l1r, l2s, l2r, l3s, l3r, l4s, l4r, prs, prr, rss, rsr,
):
    seq, head = lax.axis_index("seq"), lax.axis_index("head")
    seqs, heads = 64, 8
    x, a, b = seq // 16, (seq // 4) % 4, seq % 4
    toks, feat = q_in.shape
    local_heads = feat // HW

    sources = (q_hbm, k_hbm, v_hbm, ld_hbm, beta_hbm, taps_hbm, gain_hbm, w_hbm)
    inside = (q_in, k_in, v_in, ld_in, beta_in, taps_in, gain_in, w_in)
    loads = [
        pltpu.make_async_copy(src, dst, local_sem.at[i])
        for i, (src, dst) in enumerate(zip(sources, inside))
    ]
    for load in loads:
        load.start()

    other = head + 1 - 2 * (head % 2)

    def across(d):
        return (head + 2 * d) % heads

    def at1(d):
        return seq - b + (b + d) % 4

    def at2(d):
        return seq - 4 * a + 4 * ((a + d) % 4)

    def at3(d):
        return seq - 16 * x + 16 * ((x + d) % 4)

    after, before = (seq + 1) % seqs, (seq + seqs - 1) % seqs
    barrier = pltpu.get_barrier_semaphore()
    greet = [(after, head), (before, head)]
    greet += [(at(d), head) for at in (at1, at2, at3) for d in (1, 2, 3)]
    greet += [(seq, other)] + [(seq, across(d)) for d in (1, 2, 3)]
    for device in greet:
        pl.semaphore_signal(barrier, inc=1, device_id=device, device_id_type=MESH)

    def remote(src, dst, send, recv, device):
        return pltpu.make_async_remote_copy(
            src_ref=src, dst_ref=dst, send_sem=send, recv_sem=recv, device_id=device, device_id_type=MESH
        )

    def go(copies, when=None):
        @pl.when(seq >= 0 if when is None else when)
        def _():
            for copy in copies:
                copy.start()

    pl.semaphore_wait(barrier, len(greet))
    rim_copies = [
        remote(src.at[pl.ds(toks - RIM, RIM), :], rims.at[i], rim_send.at[i], rim_recv.at[i], (after, head))
        for i, src in enumerate((q_hbm, k_hbm, v_hbm))
    ]
    go(rim_copies)

    row, col = iotas(toks)
    inclusive = row >= col
    strict = row > col
    eye = (row == col).astype(F32)
    for load in loads[3:7]:
        load.wait()
    cum = mm(inclusive.astype(BF16), ld_in[...])
    middle = cum[toks // 2 - 1 : toks // 2, :]
    last = cum[toks - 1 : toks, :]
    grow = jnp.exp(cum - middle)
    shrink = jnp.exp(middle - cum)
    from_start = jnp.exp(middle)
    to_end = jnp.exp(last - middle)
    loss = jnp.exp(last) - 1.0
    strength = 1.0 / (1.0 + jnp.exp(-beta_in[...]))

    for load in loads[:3]:
        load.wait()
    raws = (q_in, k_in, v_in)
    for i in range(3):
        ext[i, 0:RIM, :] = jnp.zeros((RIM, feat), F32)
        ext[i, RIM : RIM + toks, :] = raws[i][...].astype(F32)
    conved = [conv_silu(ext, taps_in, i, toks) for i in range(3)]


    def head_parts(parts_of, h, rows):
        cols = slice(h * HW, (h + 1) * HW)
        q_h, k_h, v_h = (part[:, cols] for part in parts_of)
        q_h = q_h * lax.rsqrt(jnp.sum(q_h * q_h, axis=-1, keepdims=True) + 1e-06)
        k_h = k_h * lax.rsqrt(jnp.sum(k_h * k_h, axis=-1, keepdims=True) + 1e-06)
        return k_h * grow[:rows, cols], k_h * shrink[:rows, cols], q_h * grow[:rows, cols], v_h

    betas, firsts, lowers = [], [], []
    for h in range(local_heads):
        betas.append(jnp.transpose(jnp.broadcast_to(strength[h : h + 1, :], (HW, toks))))
        firsts.append(head_parts(conved, h, toks))
        lower = mm_full(firsts[h][0], jnp.transpose(firsts[h][1])) * betas[h]
        lowers.append(jnp.where(strict & (col >= EDGE), lower, 0.0))
    for h, inv in enumerate(unit_lower_inverses(lowers, row, col)):
        qeff[h] = inv

    @pl.when(seq >= 0)
    def _():
        for copy in rim_copies:
            copy.wait_recv()

    for i in range(3):
        ext[i, 0:RIM, :] = jnp.where(seq > 0, rims[i].astype(F32), 0.0)
    edges = [conv_silu(ext, taps_in, i, EDGE) for i in range(3)]
    queries, keys, scores, sides, corners = [], [], [], [], []
    for h in range(local_heads):
        cols = slice(h * HW, (h + 1) * HW)
        key_pos, key_neg, query_pos, v_h = (
            jnp.concatenate([edge, part[EDGE:]], axis=0)
            for edge, part in zip(head_parts(edges, h, EDGE), firsts[h])
        )
        both = mm_full(jnp.concatenate([key_pos, query_pos], axis=0), jnp.transpose(key_neg))
        corners.append(jnp.where(strict & (col < EDGE), both[:toks] * betas[h], 0.0))
        scores.append(jnp.where(inclusive, both[toks:], 0.0))
        queries.append(query_pos * from_start[:, cols])
        keys.append(jnp.transpose(key_neg * to_end[:, cols]))
        sides.append(jnp.concatenate([key_pos * from_start[:, cols] * betas[h], v_h * betas[h]], axis=1))
    edge_sols = [side[:EDGE] for side in sides]
    for j in range(EDGE - 1):
        edge_sols = [
            sol - corner[:EDGE, j : j + 1] * sol[j : j + 1, :] for sol, corner in zip(edge_sols, corners)
        ]
    below = [
        mm_full(corner, jnp.concatenate([sol, jnp.zeros((toks - EDGE, 2 * HW), F32)], axis=0))
        for corner, sol in zip(corners, edge_sols)
    ]
    solved = [
        mm_full(inv, jnp.concatenate([sol, side[EDGE:] - low[EDGE:]], axis=0))
        for inv, sol, side, low in zip([qeff[h] for h in range(local_heads)], edge_sols, sides, below)
    ]
    for h in range(local_heads):
        cols = slice(h * HW, (h + 1) * HW)
        outs = mm_full(jnp.concatenate([scores[h], keys[h]], axis=0), solved[h])
        qeff[h] = queries[h] - outs[:toks, :HW]
        intra[h] = outs[:toks, HW:]
        e1_send[h, :, :HW] = (eye * loss[:, cols] - outs[toks:, :HW]).astype(BF16)
        e1_send[h, :, HW:] = outs[toks:, HW:].astype(BF16)

    def exchange(send_of, recv, mine, at, sends, recvs):
        out, arrive = [], []
        for d in (2, 1, 3):
            ends = (sends.at[d - 1], recvs.at[d - 1], (at(d), head))
            out.append(remote(send_of((mine + d) % 4), recv.at[mine], *ends))
            slot = (mine + 4 - d) % 4
            arrive.append(remote(send_of(slot), recv.at[slot], *ends))
        go(out)
        return out, arrive

    out1, arrive1 = exchange(lambda h: e1_send.at[h], e1_recv, b, at1, l1s, l1r)
    e1_recv[b] = e1_send[b]
    for copy in arrive1:
        copy.wait_recv()
    maps1 = [e1_recv[0].astype(F32)]
    for n in (1, 2, 3):
        maps1.append(compose(e1_recv[n], maps1[-1]))

    e2_send[...] = maps1[3].astype(BF16)
    out2, arrive2 = exchange(lambda h: e2_send, e2_recv, a, at2, l2s, l2r)
    e2_recv[a] = e2_send[...]
    for copy in arrive2:
        copy.wait_recv()
    run = e2_recv[0].astype(F32)
    before2 = jnp.zeros_like(run)
    for n in (1, 2, 3):
        before2 = jnp.where(a == n, run, before2)
        run = compose(e2_recv[n], run)

    n3_send[...] = run[:, HW:].astype(BF16)
    e3_send[...] = run[:, :HW].astype(BF16)
    out3n = [remote(n3_send, n3_recv.at[x], l3s.at[d - 1], l3r.at[d - 1], (at3(d), head)) for d in (1, 2, 3)]
    out3e = [remote(e3_send, e3_recv.at[x], l3s.at[d + 2], l3r.at[d + 2], (at3(d), head)) for d in (1, 2)]
    came3n = [
        remote(n3_send, n3_recv.at[(x + 4 - d) % 4], l3s.at[d - 1], l3r.at[d - 1], (at3(d), head)) for d in (1, 2, 3)
    ]
    came3e = [
        remote(e3_send, e3_recv.at[(x + 4 - d) % 4], l3s.at[d + 2], l3r.at[d + 2], (at3(d), head)) for d in (1, 2)
    ]
    for d in (2, 1, 3):
        pl.when(x + d < 4)(out3n[d - 1].start)
    for d in (2, 1):
        pl.when((x >= 1) & (x + d < 4))(out3e[d - 1].start)
    for d in (1, 2, 3):
        pl.when(x >= d)(came3n[d - 1].wait_recv)
    for d in (1, 2):
        pl.when(x >= d + 1)(came3e[d - 1].wait_recv)
    state = n3_recv[0].astype(F32)
    entering = jnp.zeros_like(state)
    entering = jnp.where(x == 1, state, entering)
    for n in (1, 2):
        state = state + mm_exact_left(e3_recv[n], state) + n3_recv[n].astype(F32)
        entering = jnp.where(x == n + 1, state, entering)
    entering = entering + mm_full(before2[:, :HW], entering) + before2[:, HW:]
    s4_send[0] = entering.astype(BF16)
    for n in (1, 2, 3):
        s4_send[n] = (entering + mm_full(maps1[n - 1][:, :HW], entering) + maps1[n - 1][:, HW:]).astype(BF16)

    out4, arrive4 = exchange(lambda h: s4_send.at[h], s4_recv, b, at1, l4s, l4r)
    s4_recv[b] = s4_send[b]
    for copy in arrive4:
        copy.wait_recv()
    normed = []
    for h in range(local_heads):
        q_hi, q_lo = halves(qeff[h])
        state_h = s4_recv[h]
        attended = intra[h] + mm(
            jnp.concatenate([q_hi, q_lo], axis=1), jnp.concatenate([state_h, state_h], axis=0)
        )
        scale = lax.rsqrt(jnp.mean(attended * attended, axis=-1, keepdims=True) + 1e-06)
        normed.append((attended * scale * gain_in[:, h * HW : (h + 1) * HW]).astype(BF16))
    normed = jnp.concatenate(normed, axis=1)

    loads[7].wait()
    width = w_in.shape[1] // CHUNKS
    rows = toks // heads
    core, place = head % 2, head // 2
    pairs, spread, coming = [], [], []
    for c in range(CHUNKS):
        cols = slice(c * width, (c + 1) * width)
        partial = mm(normed, w_in[:, cols]).astype(BF16)
        for t in range(heads):
            parts[t % 2, (t // 2) * rows : (t // 2 + 1) * rows, cols] = partial[t * rows : (t + 1) * rows]
        pairs.append(remote(parts.at[1 - core, :, cols], paired.at[:, cols], prs.at[c], prr.at[c], (seq, other)))
        go(pairs[-1:])
    for c in range(CHUNKS):
        cols = slice(c * width, (c + 1) * width)
        pairs[c].wait_recv()
        both = parts[core, :, cols].astype(F32) + paired[:, cols].astype(F32)
        for t in range(4):
            summed[t, :, cols] = both[t * rows : (t + 1) * rows].astype(BF16)
        for d in (2, 1, 3):
            to, source = (place + d) % 4, (place + 4 - d) % 4
            ends = (rss.at[c, d - 1], rsr.at[c, d - 1], (seq, across(d)))
            spread.append(remote(summed.at[to, :, cols], landed.at[place, :, cols], *ends))
            coming.append(remote(summed.at[to, :, cols], landed.at[source, :, cols], *ends))
        go(spread[-3:])
    for c in range(CHUNKS):
        cols = slice(c * width, (c + 1) * width)
        total = summed[place, :, cols].astype(F32)
        for copy in coming[3 * c : 3 * c + 3]:
            copy.wait_recv()
        for d in (1, 2, 3):
            total = total + landed[(place + d) % 4, :, cols].astype(F32)
        o_ref[:, cols] = total.astype(BF16)
    for copy in rim_copies + out1 + out2 + out4 + pairs + spread:
        copy.wait_send()
    for d in (1, 2, 3):
        pl.when(x + d < 4)(out3n[d - 1].wait_send)
    for d in (1, 2):
        pl.when((x >= 1) & (x + d < 4))(out3e[d - 1].wait_send)


def body(q_raw, k_raw, v_raw, log_decay, beta_logit, conv_weight, norm_gain, out_weight):
    toks, feat = q_raw.shape
    local_heads = feat // HW
    heads = lax.axis_size("head")
    width = out_weight.shape[1]
    dma = pltpu.SemaphoreType.DMA
    gain = norm_gain.reshape(1, feat)
    operands = (q_raw, k_raw, v_raw, log_decay, beta_logit, conv_weight, gain, out_weight)
    scratch = [pltpu.VMEM(op.shape, op.dtype) for op in operands]
    scratch += [
        pltpu.VMEM((3, RIM, feat), BF16),
        pltpu.VMEM((3, RIM + toks, feat), F32),
        pltpu.VMEM((local_heads, toks, HW), F32),
        pltpu.VMEM((local_heads, toks, HW), F32),
        pltpu.VMEM((4, HW, 2 * HW), BF16),
        pltpu.VMEM((4, HW, 2 * HW), BF16),
        pltpu.VMEM((HW, 2 * HW), BF16),
        pltpu.VMEM((4, HW, 2 * HW), BF16),
        pltpu.VMEM((HW, HW), BF16),
        pltpu.VMEM((4, HW, HW), BF16),
        pltpu.VMEM((HW, HW), BF16),
        pltpu.VMEM((4, HW, HW), BF16),
        pltpu.VMEM((4, HW, HW), BF16),
        pltpu.VMEM((4, HW, HW), BF16),
        pltpu.VMEM((2, toks // 2, width), BF16),
        pltpu.VMEM((toks // 2, width), BF16),
        pltpu.VMEM((4, toks // heads, width), BF16),
        pltpu.VMEM((4, toks // heads, width), BF16),
        dma((len(operands),)), dma((3,)), dma((3,)),
        dma((3,)), dma((3,)), dma((3,)), dma((3,)), dma((5,)), dma((5,)), dma((3,)), dma((3,)),
        dma((CHUNKS,)), dma((CHUNKS,)), dma((CHUNKS, 3)), dma((CHUNKS, 3)),
    ]
    return pl.pallas_call(
        kernel,
        out_shape=jax.ShapeDtypeStruct((toks // heads, width), BF16),
        in_specs=[pl.BlockSpec(memory_space=pltpu.HBM)] * len(operands),
        out_specs=pl.BlockSpec(memory_space=pltpu.VMEM),
        scratch_shapes=scratch,
        compiler_params=pltpu.CompilerParams(
            collective_id=0, has_side_effects=True, vmem_limit_bytes=48 * 2**20
        ),
        cost_estimate=pl.CostEstimate(flops=2 * 10**9, bytes_accessed=3 * 10**6, transcendentals=10**6),
    )(*[pltpu.with_memory_space_constraint(op, pltpu.HBM) for op in operands])


def solution(mesh):
    in_specs = (
        P("seq", "head"),
        P("seq", "head"),
        P("seq", "head"),
        P("seq", "head"),
        P("head", "seq"),
        P(None, None, "head"),
        P("head"),
        P("head", None),
    )
    out_specs = P(("seq", "head"), None)
    return jax.shard_map(body, mesh=mesh, in_specs=in_specs, out_specs=out_specs, check_vma=False)
```

```python
import functools

import jax
import jax.numpy as jnp
from jax import lax
from jax.experimental import pallas as pl
from jax.experimental.pallas import tpu as pltpu
from jax.sharding import PartitionSpec as P

MESH = pl.DeviceIdType.MESH
F32 = jnp.float32
BF16 = jnp.bfloat16
HW = 128
CONV = 4
RIM = 16
EDGE = 8
CHUNKS = 1


def halves(value):
    high = value.astype(BF16)
    return high, (value - high.astype(F32)).astype(BF16)


def mm(a, b):
    return jnp.dot(a, b, preferred_element_type=F32)


def mm_full(a, b):
    a_hi, a_lo = halves(a)
    b_hi, b_lo = halves(b)
    wide = mm(jnp.concatenate([a_hi, a_lo], axis=1), jnp.concatenate([b_hi, b_hi], axis=0))
    return wide + mm(a_hi, b_lo)


def mm_exact_left(a_bf, b):
    b_hi, b_lo = halves(b)
    return mm(jnp.concatenate([a_bf, a_bf], axis=1), jnp.concatenate([b_hi, b_lo], axis=0))


def iotas(n):
    return lax.broadcasted_iota(jnp.int32, (n, n), 0), lax.broadcasted_iota(jnp.int32, (n, n), 1)


def unit_lower_inverses(lowers, row, col):
    differ = jnp.bitwise_xor(row, col)
    eye = (row == col).astype(F32)
    invs = [eye - jnp.where(differ == 1, low, 0.0) for low in lowers]
    level = 1
    while (2 << level) <= lowers[0].shape[0]:
        pick = lax.shift_right_logical(differ, level) == 1
        mids = [mm_full(jnp.where(pick, low, 0.0), inv) for low, inv in zip(lowers, invs)]
        invs = [inv - mm_full(inv, mid) for inv, mid in zip(invs, mids)]
        level += 1
    return invs


def conv_silu(ext, taps, i, rows):
    total = jnp.zeros((rows, ext.shape[2]), F32)
    for j in range(CONV):
        first = RIM - (CONV - 1) + j
        total = total + ext[i, first : first + rows, :] * taps[i, j : j + 1, :]
    return total / (1.0 + jnp.exp(-total))


def compose(later_bf, earlier):
    width = earlier.shape[0]
    return earlier + mm_exact_left(later_bf[:, :width], earlier) + later_bf.astype(F32)


def kernel(
    q_hbm, k_hbm, v_hbm, ld_hbm, beta_hbm, taps_hbm, gain_hbm, w_hbm,
    o_ref,
    q_in, k_in, v_in, ld_in, beta_in, taps_in, gain_in, w_in,
    rims, ext, qeff, intra,
    e1_send, e1_recv, e2_send, e2_recv, n3_send, n3_recv, e3_send, e3_recv, s4_send, s4_recv,
    parts, paired, summed, landed,
    local_sem, rim_send, rim_recv,
    l1s, l1r, l2s, l2r, l3s, l3r, l4s, l4r, prs, prr, rss, rsr,
):
    seq, head = lax.axis_index("seq"), lax.axis_index("head")
    seqs, heads = 64, 8
    x, a, b = seq // 16, (seq // 4) % 4, seq % 4
    toks, feat = q_in.shape
    local_heads = feat // HW

    sources = (q_hbm, k_hbm, v_hbm, ld_hbm, beta_hbm, taps_hbm, gain_hbm, w_hbm)
    inside = (q_in, k_in, v_in, ld_in, beta_in, taps_in, gain_in, w_in)
    loads = [
        pltpu.make_async_copy(src, dst, local_sem.at[i])
        for i, (src, dst) in enumerate(zip(sources, inside))
    ]
    for load in loads:
        load.start()

    other = head + 1 - 2 * (head % 2)

    def across(d):
        return (head + 2 * d) % heads

    def at1(d):
        return seq - b + (b + d) % 4

    def at2(d):
        return seq - 4 * a + 4 * ((a + d) % 4)

    def at3(d):
        return seq - 16 * x + 16 * ((x + d) % 4)

    after, before = (seq + 1) % seqs, (seq + seqs - 1) % seqs
    barrier = pltpu.get_barrier_semaphore()
    greet = [(after, head), (before, head)]
    greet += [(at(d), head) for at in (at1, at2, at3) for d in (1, 2, 3)]
    greet += [(seq, other)] + [(seq, across(d)) for d in (1, 2, 3)]
    for device in greet:
        pl.semaphore_signal(barrier, inc=1, device_id=device, device_id_type=MESH)

    def remote(src, dst, send, recv, device):
        return pltpu.make_async_remote_copy(
            src_ref=src, dst_ref=dst, send_sem=send, recv_sem=recv, device_id=device, device_id_type=MESH
        )

    def go(copies, when=None):
        @pl.when(seq >= 0 if when is None else when)
        def _():
            for copy in copies:
                copy.start()

    pl.semaphore_wait(barrier, len(greet))
    rim_copies = [
        remote(src.at[pl.ds(toks - RIM, RIM), :], rims.at[i], rim_send.at[i], rim_recv.at[i], (after, head))
        for i, src in enumerate((q_hbm, k_hbm, v_hbm))
    ]
    go(rim_copies)

    row, col = iotas(toks)
    inclusive = row >= col
    strict = row > col
    eye = (row == col).astype(F32)
    for load in loads[3:7]:
        load.wait()
    cum = mm(inclusive.astype(BF16), ld_in[...])
    middle = cum[toks // 2 - 1 : toks // 2, :]
    last = cum[toks - 1 : toks, :]
    grow = jnp.exp(cum - middle)
    shrink = jnp.exp(middle - cum)
    from_start = jnp.exp(middle)
    to_end = jnp.exp(last - middle)
    loss = jnp.exp(last) - 1.0
    strength = 1.0 / (1.0 + jnp.exp(-beta_in[...]))

    for load in loads[:3]:
        load.wait()
    raws = (q_in, k_in, v_in)
    for i in range(3):
        ext[i, 0:RIM, :] = jnp.zeros((RIM, feat), F32)
        ext[i, RIM : RIM + toks, :] = raws[i][...].astype(F32)
    conved = [conv_silu(ext, taps_in, i, toks) for i in range(3)]


    def head_parts(parts_of, h, rows):
        cols = slice(h * HW, (h + 1) * HW)
        q_h, k_h, v_h = (part[:, cols] for part in parts_of)
        q_h = q_h * lax.rsqrt(jnp.sum(q_h * q_h, axis=-1, keepdims=True) + 1e-06)
        k_h = k_h * lax.rsqrt(jnp.sum(k_h * k_h, axis=-1, keepdims=True) + 1e-06)
        return k_h * grow[:rows, cols], k_h * shrink[:rows, cols], q_h * grow[:rows, cols], v_h

    betas, firsts, lowers = [], [], []
    for h in range(local_heads):
        betas.append(jnp.transpose(jnp.broadcast_to(strength[h : h + 1, :], (HW, toks))))
        firsts.append(head_parts(conved, h, toks))
        lower = mm_full(firsts[h][0], jnp.transpose(firsts[h][1])) * betas[h]
        lowers.append(jnp.where(strict & (col >= EDGE), lower, 0.0))
    for h, inv in enumerate(unit_lower_inverses(lowers, row, col)):
        qeff[h] = inv

    @pl.when(seq >= 0)
    def _():
        for copy in rim_copies:
            copy.wait_recv()

    for i in range(3):
        ext[i, 0:RIM, :] = jnp.where(seq > 0, rims[i].astype(F32), 0.0)
    edges = [conv_silu(ext, taps_in, i, EDGE) for i in range(3)]
    queries, keys, scores, sides, corners = [], [], [], [], []
    for h in range(local_heads):
        cols = slice(h * HW, (h + 1) * HW)
        key_pos, key_neg, query_pos, v_h = (
            jnp.concatenate([edge, part[EDGE:]], axis=0)
            for edge, part in zip(head_parts(edges, h, EDGE), firsts[h])
        )
        both = mm_full(jnp.concatenate([key_pos, query_pos], axis=0), jnp.transpose(key_neg))
        corners.append(jnp.where(strict & (col < EDGE), both[:toks] * betas[h], 0.0))
        scores.append(jnp.where(inclusive, both[toks:], 0.0))
        queries.append(query_pos * from_start[:, cols])
        keys.append(jnp.transpose(key_neg * to_end[:, cols]))
        sides.append(jnp.concatenate([key_pos * from_start[:, cols] * betas[h], v_h * betas[h]], axis=1))
    edge_sols = [side[:EDGE] for side in sides]
    for j in range(EDGE - 1):
        edge_sols = [
            sol - corner[:EDGE, j : j + 1] * sol[j : j + 1, :] for sol, corner in zip(edge_sols, corners)
        ]
    below = [
        mm_full(corner, jnp.concatenate([sol, jnp.zeros((toks - EDGE, 2 * HW), F32)], axis=0))
        for corner, sol in zip(corners, edge_sols)
    ]
    solved = [
        mm_full(inv, jnp.concatenate([sol, side[EDGE:] - low[EDGE:]], axis=0))
        for inv, sol, side, low in zip([qeff[h] for h in range(local_heads)], edge_sols, sides, below)
    ]
    for h in range(local_heads):
        cols = slice(h * HW, (h + 1) * HW)
        outs = mm_full(jnp.concatenate([scores[h], keys[h]], axis=0), solved[h])
        qeff[h] = queries[h] - outs[:toks, :HW]
        intra[h] = outs[:toks, HW:]
        e1_send[h, :, :HW] = (eye * loss[:, cols] - outs[toks:, :HW]).astype(BF16)
        e1_send[h, :, HW:] = outs[toks:, HW:].astype(BF16)

    def exchange(send_of, recv, mine, at, sends, recvs):
        out, arrive = [], []
        for d in (2, 1, 3):
            ends = (sends.at[d - 1], recvs.at[d - 1], (at(d), head))
            out.append(remote(send_of((mine + d) % 4), recv.at[mine], *ends))
            slot = (mine + 4 - d) % 4
            arrive.append(remote(send_of(slot), recv.at[slot], *ends))
        go(out)
        return out, arrive

    out1, arrive1 = exchange(lambda h: e1_send.at[h], e1_recv, b, at1, l1s, l1r)
    e1_recv[b] = e1_send[b]
    for copy in arrive1:
        copy.wait_recv()
    maps1 = [e1_recv[0].astype(F32)]
    for n in (1, 2, 3):
        maps1.append(compose(e1_recv[n], maps1[-1]))

    e2_send[...] = maps1[3].astype(BF16)
    out2, arrive2 = [], []
    for i in range(3):
        target, source = i + (i + 4 - a) // 4, (a + i + 1) % 4
        d, gap = (target + 4 - a) % 4, (a + 4 - source) % 4
        out2.append(
            remote(e2_send, e2_recv.at[a], l2s.at[d - 1], l2r.at[d - 1], (seq - 4 * a + 4 * target, head))
        )
        arrive2.append(
            remote(e2_send, e2_recv.at[source], l2s.at[gap - 1], l2r.at[gap - 1], (seq - 4 * a + 4 * source, head))
        )
    go(out2[:1])
    go(out2[1:2])
    go(out2[2:])
    e2_recv[a] = e2_send[...]
    for copy in arrive2:
        copy.wait_recv()
    run = e2_recv[0].astype(F32)
    before2 = jnp.zeros_like(run)
    for n in (1, 2, 3):
        before2 = jnp.where(a == n, run, before2)
        run = compose(e2_recv[n], run)

    n3_send[...] = run[:, HW:].astype(BF16)
    e3_send[...] = run[:, :HW].astype(BF16)
    out3n = [remote(n3_send, n3_recv.at[x], l3s.at[d - 1], l3r.at[d - 1], (at3(d), head)) for d in (1, 2, 3)]
    out3e = [remote(e3_send, e3_recv.at[x], l3s.at[d + 2], l3r.at[d + 2], (at3(d), head)) for d in (1, 2)]
    came3n = [
        remote(n3_send, n3_recv.at[(x + 4 - d) % 4], l3s.at[d - 1], l3r.at[d - 1], (at3(d), head)) for d in (1, 2, 3)
    ]
    came3e = [
        remote(e3_send, e3_recv.at[(x + 4 - d) % 4], l3s.at[d + 2], l3r.at[d + 2], (at3(d), head)) for d in (1, 2)
    ]
    for d in (2, 1, 3):
        pl.when(x + d < 4)(out3n[d - 1].start)
    for d in (2, 1):
        pl.when((x >= 1) & (x + d < 4))(out3e[d - 1].start)
    for d in (1, 2, 3):
        pl.when(x >= d)(came3n[d - 1].wait_recv)
    for d in (1, 2):
        pl.when(x >= d + 1)(came3e[d - 1].wait_recv)
    state = n3_recv[0].astype(F32)
    entering = jnp.zeros_like(state)
    entering = jnp.where(x == 1, state, entering)
    for n in (1, 2):
        state = state + mm_exact_left(e3_recv[n], state) + n3_recv[n].astype(F32)
        entering = jnp.where(x == n + 1, state, entering)
    entering = entering + mm_full(before2[:, :HW], entering) + before2[:, HW:]
    s4_send[0] = entering.astype(BF16)
    for n in (1, 2, 3):
        s4_send[n] = (entering + mm_full(maps1[n - 1][:, :HW], entering) + maps1[n - 1][:, HW:]).astype(BF16)

    out4, arrive4 = exchange(lambda h: s4_send.at[h], s4_recv, b, at1, l4s, l4r)
    s4_recv[b] = s4_send[b]
    for copy in arrive4:
        copy.wait_recv()
    normed = []
    for h in range(local_heads):
        q_hi, q_lo = halves(qeff[h])
        state_h = s4_recv[h]
        attended = intra[h] + mm(
            jnp.concatenate([q_hi, q_lo], axis=1), jnp.concatenate([state_h, state_h], axis=0)
        )
        scale = lax.rsqrt(jnp.mean(attended * attended, axis=-1, keepdims=True) + 1e-06)
        normed.append((attended * scale * gain_in[:, h * HW : (h + 1) * HW]).astype(BF16))
    normed = jnp.concatenate(normed, axis=1)

    loads[7].wait()
    width = w_in.shape[1] // CHUNKS
    rows = toks // heads
    core, place = head % 2, head // 2
    pairs, spread, coming = [], [], []
    for c in range(CHUNKS):
        cols = slice(c * width, (c + 1) * width)
        partial = mm(normed, w_in[:, cols]).astype(BF16)
        for t in range(heads):
            parts[t % 2, (t // 2) * rows : (t // 2 + 1) * rows, cols] = partial[t * rows : (t + 1) * rows]
        pairs.append(remote(parts.at[1 - core, :, cols], paired.at[:, cols], prs.at[c], prr.at[c], (seq, other)))
        go(pairs[-1:])
    for c in range(CHUNKS):
        cols = slice(c * width, (c + 1) * width)
        pairs[c].wait_recv()
        both = parts[core, :, cols].astype(F32) + paired[:, cols].astype(F32)
        for t in range(4):
            summed[t, :, cols] = both[t * rows : (t + 1) * rows].astype(BF16)
        for d in (2, 1, 3):
            to, source = (place + d) % 4, (place + 4 - d) % 4
            ends = (rss.at[c, d - 1], rsr.at[c, d - 1], (seq, across(d)))
            spread.append(remote(summed.at[to, :, cols], landed.at[place, :, cols], *ends))
            coming.append(remote(summed.at[to, :, cols], landed.at[source, :, cols], *ends))
        go(spread[-3:])
    for c in range(CHUNKS):
        cols = slice(c * width, (c + 1) * width)
        total = summed[place, :, cols].astype(F32)
        for copy in coming[3 * c : 3 * c + 3]:
            copy.wait_recv()
        for d in (1, 2, 3):
            total = total + landed[(place + d) % 4, :, cols].astype(F32)
        o_ref[:, cols] = total.astype(BF16)
    for copy in rim_copies + out1 + out2 + out4 + pairs + spread:
        copy.wait_send()
    for d in (1, 2, 3):
        pl.when(x + d < 4)(out3n[d - 1].wait_send)
    for d in (1, 2):
        pl.when((x >= 1) & (x + d < 4))(out3e[d - 1].wait_send)


def body(q_raw, k_raw, v_raw, log_decay, beta_logit, conv_weight, norm_gain, out_weight):
    toks, feat = q_raw.shape
    local_heads = feat // HW
    heads = lax.axis_size("head")
    width = out_weight.shape[1]
    dma = pltpu.SemaphoreType.DMA
    gain = norm_gain.reshape(1, feat)
    operands = (q_raw, k_raw, v_raw, log_decay, beta_logit, conv_weight, gain, out_weight)
    scratch = [pltpu.VMEM(op.shape, op.dtype) for op in operands]
    scratch += [
        pltpu.VMEM((3, RIM, feat), BF16),
        pltpu.VMEM((3, RIM + toks, feat), F32),
        pltpu.VMEM((local_heads, toks, HW), F32),
        pltpu.VMEM((local_heads, toks, HW), F32),
        pltpu.VMEM((4, HW, 2 * HW), BF16),
        pltpu.VMEM((4, HW, 2 * HW), BF16),
        pltpu.VMEM((HW, 2 * HW), BF16),
        pltpu.VMEM((4, HW, 2 * HW), BF16),
        pltpu.VMEM((HW, HW), BF16),
        pltpu.VMEM((4, HW, HW), BF16),
        pltpu.VMEM((HW, HW), BF16),
        pltpu.VMEM((4, HW, HW), BF16),
        pltpu.VMEM((4, HW, HW), BF16),
        pltpu.VMEM((4, HW, HW), BF16),
        pltpu.VMEM((2, toks // 2, width), BF16),
        pltpu.VMEM((toks // 2, width), BF16),
        pltpu.VMEM((4, toks // heads, width), BF16),
        pltpu.VMEM((4, toks // heads, width), BF16),
        dma((len(operands),)), dma((3,)), dma((3,)),
        dma((3,)), dma((3,)), dma((3,)), dma((3,)), dma((5,)), dma((5,)), dma((3,)), dma((3,)),
        dma((CHUNKS,)), dma((CHUNKS,)), dma((CHUNKS, 3)), dma((CHUNKS, 3)),
    ]
    return pl.pallas_call(
        kernel,
        out_shape=jax.ShapeDtypeStruct((toks // heads, width), BF16),
        in_specs=[pl.BlockSpec(memory_space=pltpu.HBM)] * len(operands),
        out_specs=pl.BlockSpec(memory_space=pltpu.VMEM),
        scratch_shapes=scratch,
        compiler_params=pltpu.CompilerParams(
            collective_id=0, has_side_effects=True, vmem_limit_bytes=48 * 2**20
        ),
        cost_estimate=pl.CostEstimate(flops=2 * 10**9, bytes_accessed=3 * 10**6, transcendentals=10**6),
    )(*[pltpu.with_memory_space_constraint(op, pltpu.HBM) for op in operands])


def solution(mesh):
    in_specs = (
        P("seq", "head"),
        P("seq", "head"),
        P("seq", "head"),
        P("seq", "head"),
        P("head", "seq"),
        P(None, None, "head"),
        P("head"),
        P("head", None),
    )
    out_specs = P(("seq", "head"), None)
    return jax.shard_map(body, mesh=mesh, in_specs=in_specs, out_specs=out_specs, check_vma=False)
```
